32 devices in a mesh: groups: 1, expert: 8 (over z, y), head: 2 (over x), pair: 2 (over core).
Axes of the slice: x: 2, y: 2, z: 4, core: 2. Of those that a mesh axis runs over, the one named last changes fastest.
Arguments:
- hidden: bfloat16 [512, 4096], P(('groups', 'expert', 'pair'), 'head'), may hold values from -6 to 6
- expert_ids: int32 [512, 8], P(('groups', 'expert', 'pair')), may hold values from 0 to 15, all different within a row; in each aligned block of 32 rows (0 to 31, 32 to 63, ...) at most 32 rows name the same one
- route_weights: float32 [512, 8], P(('groups', 'expert', 'pair')), may hold values from 0.05 to 1
- w_gate: bfloat16 [16, 4096, 1024], P(('expert', 'pair'), None, 'head'), may hold values from -0.09375 to 0.09375
- w_up: bfloat16 [16, 4096, 1024], P(('expert', 'pair'), None, 'head'), may hold values from -0.09375 to 0.09375
- w_down: bfloat16 [16, 1024, 4096], P(('expert', 'pair'), 'head'), may hold values from -0.1875 to 0.1875
Outputs:
- moe_out: bfloat16 [512, 4096], P(('groups', 'expert', 'pair'), 'head')
The draws below stay inside these ranges and needn't reach their ends.
Inputs may be any that keep to these rules, and one draw needn't show every extreme that they name: `expert_ids`: in each aligned block of 32 rows (the rows of one device) no expert is named by more than 32 rows, a bound that some block reaches. A row names 8 different experts.
All inputs are finite; a program needn't handle non-finite values.
Results may differ from the reference program's by a relative error of at most 0.0085.
Values may be sent and summed in bfloat16 or wider, within the bound.
A program may use at most 64 MiB of HBM per device.

```python
import math
import jax
import jax.numpy as jnp
import numpy as np
from jax import lax

D = 4096
FFE = 1024
TOPK = 8
ROW_DEV = 32
EXPERTS = 16
ROWS = 512
CAP = 32
N_HEAD = 2


def steps_of(stream_key, shape, cuts, smallest, top_value):
    factor_of = 1.0
    for position, shards_of in cuts:
        heights = jax.random.uniform(jax.random.fold_in(jax.random.fold_in(stream_key, 6), position), (shards_of,), jnp.float32, smallest / len(cuts), top_value / len(cuts))
        factor_of = factor_of * jnp.repeat(jnp.exp(heights), shape[position] // shards_of).reshape((-1,) + (1,) * (len(shape) - 1 - position))
    return factor_of


def assign_block(key, own, number, rows, count, top, limit, slope):
    ranking = jax.random.permutation(key, count)
    packed, common = shares(count, rows * top, limit, slope, True), shares(count, rows * top, limit, slope, False)
    places = jnp.arange(count)

    def named(lengths, rotation):
        used = int((lengths > 0).sum())
        fixed = max(1, used // 4)
        passed = fixed + (places - fixed + rotation * (used - fixed)) % max(1, count - fixed)
        return jnp.zeros((count,), jnp.int32).at[ranking[jnp.where(places < fixed, places, passed)]].set(jnp.asarray(lengths, jnp.int32))

    lengths = jnp.where(number % 4 == 0, named(packed, number // 4), named(common, number - number // 4 - 1))
    mixed = jax.random.permutation(jax.random.fold_in(own, 3), count)
    giver, taker = mixed[0:count // 2 * 2:2], mixed[1:count // 2 * 2:2]
    room = jnp.minimum(lengths[giver] - 1, limit - lengths[taker]) // 2
    room = jnp.where((giver == ranking[0]) | (taker == ranking[0]) | (lengths[taker] == 0), 0, jnp.maximum(room, 0))
    passed = jax.random.randint(jax.random.fold_in(own, 4), (count // 2,), 0, 1 << 20) % (room + 1)
    lengths = lengths.at[giver].add(-passed).at[taker].add(passed)
    labels = jnp.searchsorted(jnp.cumsum(lengths), jnp.arange(rows * top), side="right").astype(jnp.int32)
    listing = labels.reshape(top, rows).T
    listing = listing[jax.random.permutation(jax.random.fold_in(own, 1), rows)]
    rotation = jax.random.randint(jax.random.fold_in(own, 2), (rows, 1), 0, top)
    return jnp.take_along_axis(listing, (jnp.arange(top)[None, :] + rotation) % top, axis=1)


def shares(amount, total, reach, skew, full):
    loads = [(1 << 20) // math.isqrt(rank ** skew) + 1 for rank in range(1, amount + 1)]
    largest = reach if full else min(reach, max(-(-total // amount), total * loads[0] // sum(loads)))
    least = 1 if total - largest >= amount - 1 else 0
    holding, spare = [largest] + [least] * (amount - 1), total - largest - least * (amount - 1)
    while spare > 0:
        free = [i for i in range(1, amount) if holding[i] < largest] or [i for i in range(1, amount) if holding[i] < reach]
        mass, remaining = sum([loads[i] for i in free]), spare
        for i in free:
            extra = min(reach - holding[i], max(1, remaining * loads[i] // mass), spare)
            holding[i] = holding[i] + extra
            spare = spare - extra
    return np.array(holding)


def bell_draw(rng, extent, deviation, most, shards=(), kind=jnp.bfloat16):
    array = jax.random.normal(rng, extent, jnp.float32) * deviation
    if len(shards) > 0:
        array = steps_of(rng, extent, shards, -0.22, 0.18) * array
    return jnp.clip(array, min=-most, max=most).astype(kind)


def setup_inputs(seed: int = 0, part: int = 0) -> dict:
    arg_keys = jax.random.split(jax.random.key(seed), 7)
    part_splits = jax.random.split(jax.random.fold_in(arg_keys[6], part), 7)
    hidden = bell_draw(part_splits[0], (ROWS, D), 1.0, 6.0, ((0, 16), (1, 2)))
    expert_ids_keys = jax.random.split(jax.random.fold_in(part_splits[1], 1), ROWS // ROW_DEV)
    expert_ids_turns = jax.random.permutation(jax.random.fold_in(part_splits[1], 3), ROWS // ROW_DEV)
    expert_ids = jax.vmap(lambda own, number: assign_block(jax.random.fold_in(part_splits[1], 2), own, number, ROW_DEV, EXPERTS, TOPK, CAP, 2))(expert_ids_keys, expert_ids_turns).reshape((ROWS, TOPK))
    route_weights = jnp.clip(jnp.exp(math.log(1.0) - 2.9957323 * jax.random.uniform(part_splits[2], (ROWS, TOPK), jnp.float32) ** steps_of(part_splits[2], (ROWS, TOPK), ((0, 16),), -0.2, 0.2)), 0.05, 1.0)
    w_gate = bell_draw(arg_keys[3], (EXPERTS, D, FFE), D ** -0.5, 0.09375, ((0, 16), (2, 2)))
    w_up = bell_draw(arg_keys[4], (EXPERTS, D, FFE), D ** -0.5, 0.09375, ((0, 16), (2, 2)))
    w_down = bell_draw(arg_keys[5], (EXPERTS, FFE, D), FFE ** -0.5, 0.1875, ((0, 16), (1, 2)))
    return dict(hidden=hidden, expert_ids=expert_ids, route_weights=route_weights, w_gate=w_gate, w_up=w_up, w_down=w_down)


def reference(hidden, expert_ids, route_weights, w_gate, w_up, w_down):
    total_rows = hidden.shape[0]
    block_count = total_rows // ROW_DEV
    route_span = ROW_DEV * TOPK
    block_ids = expert_ids.reshape(block_count, route_span).astype(jnp.int32)
    one_hot = (block_ids[:, :, None] == jnp.arange(EXPERTS, dtype=jnp.int32)[None, None, :]).astype(jnp.int32)
    earlier = jnp.cumsum(one_hot, axis=1) - one_hot
    slot_index = jnp.sum(earlier * one_hot, axis=2).astype(jnp.int32)
    block_index = jnp.broadcast_to(jnp.arange(block_count, dtype=jnp.int32)[:, None], (block_count, route_span))
    row_number = (block_index * ROW_DEV + jnp.arange(route_span, dtype=jnp.int32)[None, :] // TOPK).astype(jnp.int32)
    row_table = jnp.full((EXPERTS, block_count, CAP), total_rows, jnp.int32)
    row_table = row_table.at[block_ids, block_index, slot_index].set(row_number)
    weight_table = jnp.zeros((EXPERTS, block_count, CAP), jnp.float32)
    weight_table = weight_table.at[block_ids, block_index, slot_index].set(route_weights.reshape(block_count, route_span))
    padded = jnp.concatenate([hidden, jnp.zeros((1, D), hidden.dtype)], axis=0)
    local_hidden = FFE // N_HEAD

    def one_expert(totals, expert):
        row_list = row_table[expert].reshape(-1)
        gathered = padded[row_list]
        gate_acts = jnp.dot(gathered, w_gate[expert], preferred_element_type=jnp.float32)
        up_acts = jnp.dot(gathered, w_up[expert], preferred_element_type=jnp.float32)
        activated = (jax.nn.silu(gate_acts) * up_acts).astype(jnp.bfloat16)
        grouped = activated.reshape(-1, N_HEAD, local_hidden).astype(jnp.float32)
        down_groups = w_down[expert].reshape(N_HEAD, local_hidden, D).astype(jnp.float32)
        partials = jnp.einsum("nhf,hfd->hnd", grouped, down_groups, precision=lax.Precision.HIGHEST).astype(jnp.bfloat16)
        partials = lax.optimization_barrier(partials)
        expert_out = jnp.sum(partials.astype(jnp.float32), axis=0)
        scaled = weight_table[expert].reshape(-1)[:, None] * expert_out
        return totals.at[row_list].add(scaled), None

    totals, unused = lax.scan(one_expert, jnp.zeros((total_rows + 1, D), jnp.float32), jnp.arange(EXPERTS, dtype=jnp.int32))
    return totals[:total_rows].astype(jnp.bfloat16)
```

```python
import functools

import jax
import jax.numpy as jnp
from jax import lax
from jax.experimental import pallas as pl
from jax.experimental.pallas import tpu as pltpu
from jax.sharding import PartitionSpec as P

MESH = pl.DeviceIdType.MESH
LANES = 128


def flip(value, bits):
    result = value
    bit = 1
    while bit <= bits:
        if bits & bit:
            result = result + bit * (1 - 2 * ((value // bit) % 2))
        bit *= 2
    return result


def kernel(
    dims, hidden, ids, weights, gate_hbm, up_hbm, down_hbm, out,
    rows_all, table, w_gate, w_up, w_down, part, act, d2d_in, y_in, x_in, x_in2, y_in2, z_out, z_in,
    w_sem, send_sem, recv_sem,
):
    Z, H, RB = dims
    RC = 4 * RB
    WD = rows_all.shape[3]
    expert = lax.axis_index("expert")
    x = lax.axis_index("head")
    c = lax.axis_index("pair")
    z, y = expert // 2, expert % 2
    other = 1 - c
    me = expert * 2 + c

    to_y = {"expert": z * 2 + 1 - y}
    to_c = {"pair": other}

    def to_z(j):
        return {"expert": flip(z, j) * 2 + y}

    def to_x(dx):
        return {"head": (x + dx) % H}

    def from_x(dx):
        return (x + H - dx) % H

    fetches = [
        pltpu.make_async_copy(gate_hbm.at[0], w_gate, w_sem.at[0]),
        pltpu.make_async_copy(up_hbm.at[0], w_up, w_sem.at[1]),
    ]
    for s in range(2 * H):
        fetches.append(
            pltpu.make_async_copy(
                down_hbm.at[0, :, pl.ds(s * WD, WD)], w_down.at[s // 2, s % 2], w_sem.at[2 + s]
            )
        )
    for f in fetches:
        f.start()

    def block(zc, pair, yy):
        return pl.multiple_of(((zc * 2 + pair) * 2 + yy) * RB, RB)

    own = block(z, c, y)
    for p in range(2):
        rows_all[x, p, pl.ds(own, RB), :] = hidden[:, p * WD:(p + 1) * WD]
    lane = lax.broadcasted_iota(jnp.int32, (RB, LANES), 1)
    total = jnp.zeros((RB, LANES), jnp.float32)
    for k in range(ids.shape[1]):
        total = total + jnp.where(lane == ids[:, k:k + 1], weights[:, k:k + 1], 0.0)
    table[pl.ds(own, RB), :] = total

    barrier = pltpu.get_barrier_semaphore()
    peers = [to_c, to_y] + [to_z(j) for j in range(1, Z)] + [to_x(d) for d in range(1, H)]
    for peer in peers:
        pl.semaphore_signal(barrier, inc=1, device_id=peer, device_id_type=MESH)
    pl.semaphore_wait(barrier, len(peers))

    sent = []

    def send(src, dst, peer):
        i = len(sent)
        copy = pltpu.make_async_remote_copy(
            src_ref=src, dst_ref=dst, send_sem=send_sem.at[i], recv_sem=recv_sem.at[i],
            device_id=peer, device_id_type=MESH,
        )
        copy.start()
        sent.append(copy)
        return copy

    def same(ref, peer):
        return send(ref, ref, peer)

    got = {}

    for j in range(1, Z):
        got["z", j] = same(rows_all.at[x, :, pl.ds(own, RB), :], to_z(j))
        got["zw", j] = same(table.at[pl.ds(own, RB), :], to_z(j))

    def g_start(j):
        zc = flip(z, j)
        mine = block(zc, c, y)
        if j:
            got["z", j].wait_recv()
        for d in range(1, H):
            got["x", j, d] = same(rows_all.at[x, :, pl.ds(mine, RB), :], to_x(d))
        got["y", j] = same(rows_all.at[x, :, pl.ds(mine, RB), :], to_y)
        if j:
            got["zw", j].wait_recv()
        got["yw", j] = same(table.at[pl.ds(mine, RB), :], to_y)

    def g_forward(j):
        zc = flip(z, j)
        mine, theirs = block(zc, c, y), block(zc, c, 1 - y)
        for d in range(1, H):
            got["x", j, d].wait_recv()
            got["xy", j, d] = same(rows_all.at[from_x(d), 0, pl.ds(mine, RB), :], to_y)
        got["y", j].wait_recv()
        for d in range(1, H):
            got["yx", j, d] = same(rows_all.at[x, 1, pl.ds(theirs, RB), :], to_x(d))

    def g_pair(j):
        zc = flip(z, j)
        half = block(zc, c, 0)
        for d in range(1, H):
            got["xy", j, d].wait_recv()
            got["yx", j, d].wait_recv()
        got["yw", j].wait_recv()
        got["c", j] = same(rows_all.at[:, :, pl.ds(half, 2 * RB), :], to_c)
        got["cw", j] = same(table.at[pl.ds(half, 2 * RB), :], to_c)

    def compute(j):
        zc = flip(z, j)
        start = block(zc, 0, 0)
        got["c", j].wait_recv()
        got["cw", j].wait_recv()
        if j == 0:
            fetches[0].wait()
            fetches[1].wait()
        gate = jnp.zeros((RC, w_gate.shape[1]), jnp.float32)
        up = gate
        for s in range(2 * H):
            a = rows_all[s // 2, s % 2, pl.ds(start, RC), :]
            gate = gate + jnp.dot(a, w_gate[s * WD:(s + 1) * WD, :], preferred_element_type=jnp.float32)
            up = up + jnp.dot(a, w_up[s * WD:(s + 1) * WD, :], preferred_element_type=jnp.float32)
        act[...] = (gate / (1.0 + jnp.exp(-gate)) * up).astype(jnp.bfloat16)
        if j == 0:
            for f in fetches[2:]:
                f.wait()
        lanes = lax.broadcasted_iota(jnp.int32, (RC, LANES), 1)
        scale = jnp.sum(jnp.where(lanes == me, table[pl.ds(start, RC), :], 0.0), axis=1, keepdims=True)
        for s in range(2 * H):
            o = jnp.dot(act[...], w_down[s // 2, s % 2], preferred_element_type=jnp.float32)
            part[j, s // 2, s % 2] = (o * scale).astype(jnp.bfloat16)
        away = pl.multiple_of(other * 2 * RB, 2 * RB)
        got["rc", j] = send(part.at[j, :, :, pl.ds(away, 2 * RB), :], d2d_in.at[j], to_c)

    home = pl.multiple_of(c * 2 * RB, 2 * RB)
    mine_at = pl.multiple_of((c * 2 + y) * RB, RB)
    theirs_at = pl.multiple_of((c * 2 + 1 - y) * RB, RB)

    def f32(v):
        return v.astype(jnp.float32)

    def r_first(j):
        got["rc", j].wait_recv()
        for s in range(2 * H):
            h, p = s // 2, s % 2
            v = f32(part[j, h, p, pl.ds(home, 2 * RB), :]) + f32(d2d_in[j, h, p])
            part[j, h, p, pl.ds(home, 2 * RB), :] = v.astype(jnp.bfloat16)
        got["ry", j] = send(part.at[j, :, 0, pl.ds(theirs_at, RB), :], y_in.at[j], to_y)
        for d in range(1, H):
            got["rx", j, d] = send(
                part.at[j, (x + d) % H, 1, pl.ds(home, 2 * RB), :], x_in.at[j, d - 1], to_x(d)
            )

    def r_second(j):
        got["ry", j].wait_recv()
        for h in range(H):
            v = f32(part[j, h, 0, pl.ds(mine_at, RB), :]) + f32(y_in[j, h])
            part[j, h, 0, pl.ds(mine_at, RB), :] = v.astype(jnp.bfloat16)
        for d in range(1, H):
            got["rx2", j, d] = send(
                part.at[j, (x + d) % H, 0, pl.ds(mine_at, RB), :], x_in2.at[j, d - 1], to_x(d)
            )
        v = f32(part[j, x, 1, pl.ds(home, 2 * RB), :])
        for d in range(1, H):
            got["rx", j, d].wait_recv()
            v = v + f32(x_in[j, d - 1])
        part[j, x, 1, pl.ds(home, 2 * RB), :] = v.astype(jnp.bfloat16)
        got["ry2", j] = send(part.at[j, x, 1, pl.ds(theirs_at, RB), :], y_in2.at[j], to_y)

    def r_third(j):
        v = f32(part[j, x, 0, pl.ds(mine_at, RB), :])
        for d in range(1, H):
            got["rx2", j, d].wait_recv()
            v = v + f32(x_in2[j, d - 1])
        z_out[j, 0] = v.astype(jnp.bfloat16)
        v = f32(part[j, x, 1, pl.ds(mine_at, RB), :])
        got["ry2", j].wait_recv()
        v = v + f32(y_in2[j])
        z_out[j, 1] = v.astype(jnp.bfloat16)
        if j:
            got["rz", j] = send(z_out.at[j], z_in.at[j - 1], to_z(j))

    stages = [g_start, g_forward, g_pair, compute, r_first, r_second, r_third]
    for t in range(Z + len(stages) - 1):
        for s in reversed(range(len(stages))):
            if 0 <= t - s < Z:
                stages[s](t - s)

    for j in range(1, Z):
        got["rz", j].wait_recv()
    for p in range(2):
        v = f32(z_out[0, p])
        for j in range(1, Z):
            v = v + f32(z_in[j - 1, p])
        out[:, p * WD:(p + 1) * WD] = v.astype(jnp.bfloat16)
    for copy in sent:
        copy.wait_send()


def body(hidden, ids, weights, w_gate, w_up, w_down):
    E = lax.axis_size("expert")
    H = lax.axis_size("head")
    Z = E // 2
    RB, DL = hidden.shape
    WD = DL // 2
    D, F = w_gate.shape[1:]
    rows = E * 2 * RB
    copies = (Z - 1) * 2 + Z * (2 * (H - 1) + 2 + H - 1 + 2 + 1 + 1 + (H - 1) + (H - 1) + 1) + Z - 1
    vmem = pl.BlockSpec(memory_space=pltpu.VMEM)
    anyspace = pl.BlockSpec(memory_space=pl.ANY)
    bf16 = jnp.bfloat16
    X = max(H - 1, 1)
    return pl.pallas_call(
        functools.partial(kernel, (Z, H, RB)),
        out_shape=jax.ShapeDtypeStruct((RB, DL), bf16),
        in_specs=[vmem] * 3 + [anyspace] * 3,
        out_specs=vmem,
        scratch_shapes=[
            pltpu.VMEM((H, 2, rows, WD), bf16),
            pltpu.VMEM((rows, LANES), jnp.float32),
            pltpu.VMEM((D, F), bf16),
            pltpu.VMEM((D, F), bf16),
            pltpu.VMEM((H, 2, F, WD), bf16),
            pltpu.VMEM((Z, H, 2, 4 * RB, WD), bf16),
            pltpu.VMEM((4 * RB, F), bf16),
            pltpu.VMEM((Z, H, 2, 2 * RB, WD), bf16),
            pltpu.VMEM((Z, H, RB, WD), bf16),
            pltpu.VMEM((Z, X, 2 * RB, WD), bf16),
            pltpu.VMEM((Z, X, RB, WD), bf16),
            pltpu.VMEM((Z, RB, WD), bf16),
            pltpu.VMEM((Z, 2, RB, WD), bf16),
            pltpu.VMEM((Z - 1, 2, RB, WD), bf16),
            pltpu.SemaphoreType.DMA((2 + 2 * H,)),
            pltpu.SemaphoreType.DMA((copies,)),
            pltpu.SemaphoreType.DMA((copies,)),
        ],
        compiler_params=pltpu.CompilerParams(
            collective_id=0, has_side_effects=True, vmem_limit_bytes=56 * 1024 * 1024
        ),
    )(hidden, ids, weights, w_gate, w_up, w_down)


def solution(mesh):
    return jax.shard_map(
        body,
        mesh=mesh,
        in_specs=(
            P(("groups", "expert", "pair"), "head"),
            P(("groups", "expert", "pair"), None),
            P(("groups", "expert", "pair"), None),
            P(("expert", "pair"), None, "head"),
            P(("expert", "pair"), None, "head"),
            P(("expert", "pair"), "head", None),
        ),
        out_specs=P(("groups", "expert", "pair"), "head"),
        check_vma=False,
    )
```

```python
import functools

import jax
import jax.numpy as jnp
from jax import lax
from jax.experimental import pallas as pl
from jax.experimental.pallas import tpu as pltpu
from jax.sharding import PartitionSpec as P

MESH = pl.DeviceIdType.MESH
LANES = 128


def flip(value, bits):
    result = value
    bit = 1
    while bit <= bits:
        if bits & bit:
            result = result + bit * (1 - 2 * ((value // bit) % 2))
        bit *= 2
    return result


def kernel(
    dims, hidden, ids, weights, gate_hbm, up_hbm, down_hbm, out,
    rows_all, table, flipped, w_gate, w_up, w_down, part, act, d2d_in, y_in, x_in, x_in2, y_in2, z_out, z_in,
    w_sem, send_sem, recv_sem,
):
    Z, H, RB = dims
    RC = 4 * RB
    WD = rows_all.shape[3]
    expert = lax.axis_index("expert")
    x = lax.axis_index("head")
    c = lax.axis_index("pair")
    z, y = expert // 2, expert % 2
    other = 1 - c
    me = expert * 2 + c

    to_y = {"expert": z * 2 + 1 - y}
    to_c = {"pair": other}

    def to_z(j):
        return {"expert": flip(z, j) * 2 + y}

    def to_x(dx):
        return {"head": (x + dx) % H}

    def from_x(dx):
        return (x + H - dx) % H

    fetches = [
        pltpu.make_async_copy(gate_hbm.at[0], w_gate, w_sem.at[0]),
        pltpu.make_async_copy(up_hbm.at[0], w_up, w_sem.at[1]),
    ]
    for s in range(2 * H):
        fetches.append(
            pltpu.make_async_copy(
                down_hbm.at[0, :, pl.ds(s * WD, WD)], w_down.at[s // 2, s % 2], w_sem.at[2 + s]
            )
        )
    for f in fetches:
        f.start()

    def block(zc, pair, yy):
        return pl.multiple_of(((zc * 2 + pair) * 2 + yy) * RB, RB)

    own = block(z, c, y)
    for p in range(2):
        rows_all[x, p, pl.ds(own, RB), :] = hidden[:, p * WD:(p + 1) * WD]

    barrier = pltpu.get_barrier_semaphore()
    peers = [to_c, to_y] + [to_z(j) for j in range(1, Z)] + [to_x(d) for d in range(1, H)]
    for peer in peers:
        pl.semaphore_signal(barrier, inc=1, device_id=peer, device_id_type=MESH)
    pl.semaphore_wait(barrier, len(peers))

    sent = []

    def send(src, dst, peer):
        i = len(sent)
        copy = pltpu.make_async_remote_copy(
            src_ref=src, dst_ref=dst, send_sem=send_sem.at[i], recv_sem=recv_sem.at[i],
            device_id=peer, device_id_type=MESH,
        )
        copy.start()
        sent.append(copy)
        return copy

    def same(ref, peer):
        return send(ref, ref, peer)

    got = {}

    def z_send(j):
        if j == 3:
            at = block(flip(z, 2), c, y)
            got["z", j] = same(rows_all.at[x, :, pl.ds(at, RB), :], to_z(1))
        else:
            got["z", j] = same(rows_all.at[x, :, pl.ds(own, RB), :], to_z(j))

    def make_table():
        used = 2 * lax.axis_size("expert")
        line = lax.broadcasted_iota(jnp.int32, (used, RB), 0)
        total = jnp.zeros((used, RB), jnp.float32)
        for k in range(ids.shape[0]):
            total = total + jnp.where(line == ids[k:k + 1, :], weights[k:k + 1, :], 0.0)
        flipped[...] = jnp.zeros_like(flipped)
        flipped[:used, :RB] = total
        table[pl.ds(own, RB), :] = flipped[...].T[:RB, :]
        for j in range(1, Z):
            got["zw", j] = same(table.at[pl.ds(own, RB), :], to_z(j))

    def g_start(j):
        zc = flip(z, j)
        mine = block(zc, c, y)
        if j == 0:
            z_send(1)
            if Z > 2:
                z_send(2)
        else:
            got["z", j].wait_recv()
            if 2 <= j < Z - 1:
                z_send(j + 1)
        for p in range(2):
            for d in range(1, H):
                got["x", j, d, p] = same(rows_all.at[x, p, pl.ds(mine, RB), :], to_x(d))
            got["y", j, 1 - p] = same(rows_all.at[x, 1 - p, pl.ds(mine, RB), :], to_y)
        if j == 0:
            make_table()
        else:
            got["zw", j].wait_recv()
        got["yw", j] = same(table.at[pl.ds(mine, RB), :], to_y)

    def g_forward(j):
        zc = flip(z, j)
        mine, theirs = block(zc, c, y), block(zc, c, 1 - y)
        for d in range(1, H):
            got["x", j, d, 0].wait_recv()
            got["xy", j, d] = same(rows_all.at[from_x(d), 0, pl.ds(mine, RB), :], to_y)
        got["y", j, 1].wait_recv()
        for d in range(1, H):
            got["yx", j, d] = same(rows_all.at[x, 1, pl.ds(theirs, RB), :], to_x(d))

    def g_pair(j):
        zc = flip(z, j)
        mine, theirs = block(zc, c, y), block(zc, c, 1 - y)
        for d in range(1, H):
            got["x", j, d, 1].wait_recv()
        got["c", j, 0] = same(rows_all.at[:, :, pl.ds(mine, RB), :], to_c)
        got["yw", j].wait_recv()
        got["cw", j] = same(table.at[pl.ds(block(zc, c, 0), 2 * RB), :], to_c)
        got["y", j, 0].wait_recv()
        for d in range(1, H):
            got["xy", j, d].wait_recv()
            got["yx", j, d].wait_recv()
        got["c", j, 1] = same(rows_all.at[:, :, pl.ds(theirs, RB), :], to_c)

    def compute(j):
        zc = flip(z, j)
        start = block(zc, 0, 0)
        got["c", j, 0].wait_recv()
        got["c", j, 1].wait_recv()
        got["cw", j].wait_recv()
        if j == 0:
            fetches[0].wait()
            fetches[1].wait()
        gate = jnp.zeros((RC, w_gate.shape[1]), jnp.float32)
        up = gate
        for s in range(2 * H):
            a = rows_all[s // 2, s % 2, pl.ds(start, RC), :]
            gate = gate + jnp.dot(a, w_gate[s * WD:(s + 1) * WD, :], preferred_element_type=jnp.float32)
            up = up + jnp.dot(a, w_up[s * WD:(s + 1) * WD, :], preferred_element_type=jnp.float32)
        act[...] = (gate / (1.0 + jnp.exp(-gate)) * up).astype(jnp.bfloat16)
        if j == 0:
            for f in fetches[2:]:
                f.wait()
        lanes = lax.broadcasted_iota(jnp.int32, (RC, LANES), 1)
        scale = jnp.sum(jnp.where(lanes == me, table[pl.ds(start, RC), :], 0.0), axis=1, keepdims=True)
        for s in range(2 * H):
            o = jnp.dot(act[...], w_down[s // 2, s % 2], preferred_element_type=jnp.float32)
            part[j, s // 2, s % 2] = (o * scale).astype(jnp.bfloat16)
        away = pl.multiple_of(other * 2 * RB, 2 * RB)
        got["rc", j] = send(part.at[j, :, :, pl.ds(away, 2 * RB), :], d2d_in.at[j], to_c)

    home = pl.multiple_of(c * 2 * RB, 2 * RB)
    mine_at = pl.multiple_of((c * 2 + y) * RB, RB)
    theirs_at = pl.multiple_of((c * 2 + 1 - y) * RB, RB)

    def f32(v):
        return v.astype(jnp.float32)

    def r_first(j):
        got["rc", j].wait_recv()
        for s in range(2 * H):
            h, p = s // 2, s % 2
            v = f32(part[j, h, p, pl.ds(home, 2 * RB), :]) + f32(d2d_in[j, h, p])
            part[j, h, p, pl.ds(home, 2 * RB), :] = v.astype(jnp.bfloat16)
        got["ry", j] = send(part.at[j, :, 0, pl.ds(theirs_at, RB), :], y_in.at[j], to_y)
        for d in range(1, H):
            got["rx", j, d] = send(
                part.at[j, (x + d) % H, 1, pl.ds(home, 2 * RB), :], x_in.at[j, d - 1], to_x(d)
            )

    def r_second(j):
        got["ry", j].wait_recv()
        for h in range(H):
            v = f32(part[j, h, 0, pl.ds(mine_at, RB), :]) + f32(y_in[j, h])
            part[j, h, 0, pl.ds(mine_at, RB), :] = v.astype(jnp.bfloat16)
        for d in range(1, H):
            got["rx2", j, d] = send(
                part.at[j, (x + d) % H, 0, pl.ds(mine_at, RB), :], x_in2.at[j, d - 1], to_x(d)
            )
        v = f32(part[j, x, 1, pl.ds(home, 2 * RB), :])
        for d in range(1, H):
            got["rx", j, d].wait_recv()
            v = v + f32(x_in[j, d - 1])
        part[j, x, 1, pl.ds(home, 2 * RB), :] = v.astype(jnp.bfloat16)
        got["ry2", j] = send(part.at[j, x, 1, pl.ds(theirs_at, RB), :], y_in2.at[j], to_y)

    def r_third(j):
        v = f32(part[j, x, 0, pl.ds(mine_at, RB), :])
        for d in range(1, H):
            got["rx2", j, d].wait_recv()
            v = v + f32(x_in2[j, d - 1])
        z_out[j, 0] = v.astype(jnp.bfloat16)
        v = f32(part[j, x, 1, pl.ds(mine_at, RB), :])
        got["ry2", j].wait_recv()
        v = v + f32(y_in2[j])
        z_out[j, 1] = v.astype(jnp.bfloat16)
        if j:
            got["rz", j] = send(z_out.at[j], z_in.at[j - 1], to_z(j))

    steps = [(g_start, 0), (g_forward, 0), (g_start, 1)]
    for j in range(2, Z):
        steps += [(g_start, j), (g_forward, j - 1), (g_pair, j - 2)]
        steps += [(compute, j - 3), (r_first, j - 3), (r_second, j - 4), (r_third, j - 5)]
    n = Z - 1
    steps += [
        (g_forward, n), (compute, n - 2), (g_pair, n - 1), (r_first, n - 2), (r_second, n - 3),
        (compute, n - 1), (g_pair, n), (r_first, n - 1), (r_third, n - 4), (r_second, n - 2), (r_third, n - 3),
        (compute, n), (r_first, n), (r_third, n - 2), (r_second, n - 1),
    ]
    steps = [(f, j) for f, j in steps if j > 0 or (j == 0 and f not in (r_first, r_second, r_third))]
    steps += [
        (r_second, n), (r_first, 0), (r_third, n - 1), (r_third, n), (r_second, 0), (r_third, 0),
    ]
    for step, j in steps:
        step(j)

    for j in range(1, Z):
        got["rz", j].wait_recv()
    for p in range(2):
        v = f32(z_out[0, p])
        for j in range(1, Z):
            v = v + f32(z_in[j - 1, p])
        out[:, p * WD:(p + 1) * WD] = v.astype(jnp.bfloat16)
    for copy in sent:
        copy.wait_send()


def body(hidden, ids, weights, w_gate, w_up, w_down):
    E = lax.axis_size("expert")
    H = lax.axis_size("head")
    Z = E // 2
    RB, DL = hidden.shape
    ids, weights = ids.T, weights.T
    WD = DL // 2
    D, F = w_gate.shape[1:]
    rows = E * 2 * RB
    copies = 8 * Z * (H + 2)
    vmem = pl.BlockSpec(memory_space=pltpu.VMEM)
    anyspace = pl.BlockSpec(memory_space=pl.ANY)
    bf16 = jnp.bfloat16
    X = max(H - 1, 1)
    return pl.pallas_call(
        functools.partial(kernel, (Z, H, RB)),
        out_shape=jax.ShapeDtypeStruct((RB, DL), bf16),
        in_specs=[vmem] * 3 + [anyspace] * 3,
        out_specs=vmem,
        scratch_shapes=[
            pltpu.VMEM((H, 2, rows, WD), bf16),
            pltpu.VMEM((rows, LANES), jnp.float32),
            pltpu.VMEM((LANES, LANES), jnp.float32),
            pltpu.VMEM((D, F), bf16),
            pltpu.VMEM((D, F), bf16),
            pltpu.VMEM((H, 2, F, WD), bf16),
            pltpu.VMEM((Z, H, 2, 4 * RB, WD), bf16),
            pltpu.VMEM((4 * RB, F), bf16),
            pltpu.VMEM((Z, H, 2, 2 * RB, WD), bf16),
            pltpu.VMEM((Z, H, RB, WD), bf16),
            pltpu.VMEM((Z, X, 2 * RB, WD), bf16),
            pltpu.VMEM((Z, X, RB, WD), bf16),
            pltpu.VMEM((Z, RB, WD), bf16),
            pltpu.VMEM((Z, 2, RB, WD), bf16),
            pltpu.VMEM((Z - 1, 2, RB, WD), bf16),
            pltpu.SemaphoreType.DMA((2 + 2 * H,)),
            pltpu.SemaphoreType.DMA((copies,)),
            pltpu.SemaphoreType.DMA((copies,)),
        ],
        compiler_params=pltpu.CompilerParams(
            collective_id=0, has_side_effects=True, vmem_limit_bytes=56 * 1024 * 1024
        ),
    )(hidden, ids, weights, w_gate, w_up, w_down)


def solution(mesh):
    return jax.shard_map(
        body,
        mesh=mesh,
        in_specs=(
            P(("groups", "expert", "pair"), "head"),
            P(("groups", "expert", "pair"), None),
            P(("groups", "expert", "pair"), None),
            P(("expert", "pair"), None, "head"),
            P(("expert", "pair"), None, "head"),
            P(("expert", "pair"), "head", None),
        ),
        out_specs=P(("groups", "expert", "pair"), "head"),
        check_vma=False,
    )
```

```python
import functools

import jax
import jax.numpy as jnp
from jax import lax
from jax.experimental import pallas as pl
from jax.experimental.pallas import tpu as pltpu
from jax.sharding import PartitionSpec as P

MESH = pl.DeviceIdType.MESH
LANES = 128


def flip(value, bits):
    result = value
    bit = 1
    while bit <= bits:
        if bits & bit:
            result = result + bit * (1 - 2 * ((value // bit) % 2))
        bit *= 2
    return result


def kernel(
    dims, hidden, ids, weights, gate_hbm, up_hbm, down_hbm, out,
    rows_all, table, flipped, w_gate, w_up, w_down, part, act, d2d_in, y_in, x_in, x_in2, y_in2, z_out, z_in,
    w_sem, send_sem, recv_sem,
):
    Z, H, RB = dims
    RC = 4 * RB
    WD = rows_all.shape[3]
    expert = lax.axis_index("expert")
    x = lax.axis_index("head")
    c = lax.axis_index("pair")
    z, y = expert // 2, expert % 2
    other = 1 - c
    me = expert * 2 + c

    to_y = {"expert": z * 2 + 1 - y}
    to_c = {"pair": other}

    def to_z(j):
        return {"expert": flip(z, j) * 2 + y}

    def to_x(dx):
        return {"head": (x + dx) % H}

    def from_x(dx):
        return (x + H - dx) % H

    fetches = [
        pltpu.make_async_copy(gate_hbm.at[0], w_gate, w_sem.at[0]),
        pltpu.make_async_copy(up_hbm.at[0], w_up, w_sem.at[1]),
    ]
    for s in range(2 * H):
        fetches.append(
            pltpu.make_async_copy(
                down_hbm.at[0, :, pl.ds(s * WD, WD)], w_down.at[s // 2, s % 2], w_sem.at[2 + s]
            )
        )
    for f in fetches:
        f.start()

    def block(zc, pair, yy):
        return pl.multiple_of(((zc * 2 + pair) * 2 + yy) * RB, RB)

    own = block(z, c, y)
    for p in range(2):
        rows_all[x, p, pl.ds(own, RB), :] = hidden[:, p * WD:(p + 1) * WD]

    barrier = pltpu.get_barrier_semaphore()
    peers = [to_c, to_y] + [to_z(j) for j in range(1, Z)] + [to_x(d) for d in range(1, H)]
    for peer in peers:
        pl.semaphore_signal(barrier, inc=1, device_id=peer, device_id_type=MESH)
    pl.semaphore_wait(barrier, len(peers))

    sent = []

    def send(src, dst, peer):
        i = len(sent)
        copy = pltpu.make_async_remote_copy(
            src_ref=src, dst_ref=dst, send_sem=send_sem.at[i], recv_sem=recv_sem.at[i],
            device_id=peer, device_id_type=MESH,
        )
        copy.start()
        sent.append(copy)
        return copy

    def same(ref, peer):
        return send(ref, ref, peer)

    got = {}

    def z_send(j):
        if j == 3:
            at = block(flip(z, 2), c, y)
            got["z", j] = same(rows_all.at[x, :, pl.ds(at, RB), :], to_z(1))
        else:
            got["z", j] = same(rows_all.at[x, :, pl.ds(own, RB), :], to_z(j))

    def make_table():
        used = 2 * lax.axis_size("expert")
        line = lax.broadcasted_iota(jnp.int32, (used, RB), 0)
        total = jnp.zeros((used, RB), jnp.float32)
        for k in range(ids.shape[0]):
            total = total + jnp.where(line == ids[k:k + 1, :], weights[k:k + 1, :], 0.0)
        flipped[...] = jnp.zeros_like(flipped)
        flipped[:used, :RB] = total
        table[pl.ds(own, RB), :] = flipped[...].T[:RB, :]
        for j in range(1, Z):
            got["zw", j] = same(table.at[pl.ds(own, RB), :], to_z(j))

    def g_start(j):
        zc = flip(z, j)
        mine = block(zc, c, y)
        if j == 0:
            z_send(1)
            if Z > 2:
                z_send(2)
        else:
            got["z", j].wait_recv()
            if 2 <= j < Z - 1:
                z_send(j + 1)
        for p in range(2):
            for d in range(1, H):
                got["x", j, d, p] = same(rows_all.at[x, p, pl.ds(mine, RB), :], to_x(d))
            got["y", j, 1 - p] = same(rows_all.at[x, 1 - p, pl.ds(mine, RB), :], to_y)
        if j == 0:
            make_table()
        else:
            got["zw", j].wait_recv()
        got["yw", j] = same(table.at[pl.ds(mine, RB), :], to_y)

    def g_forward(j):
        zc = flip(z, j)
        mine, theirs = block(zc, c, y), block(zc, c, 1 - y)
        for d in range(1, H):
            got["x", j, d, 0].wait_recv()
            got["xy", j, d] = same(rows_all.at[from_x(d), 0, pl.ds(mine, RB), :], to_y)
        got["y", j, 1].wait_recv()
        for d in range(1, H):
            got["yx", j, d] = same(rows_all.at[x, 1, pl.ds(theirs, RB), :], to_x(d))

    def g_pair(j):
        zc = flip(z, j)
        mine, theirs = block(zc, c, y), block(zc, c, 1 - y)
        for d in range(1, H):
            got["x", j, d, 1].wait_recv()
        got["c", j, 0] = same(rows_all.at[:, :, pl.ds(mine, RB), :], to_c)
        got["yw", j].wait_recv()
        got["cw", j] = same(table.at[pl.ds(block(zc, c, 0), 2 * RB), :], to_c)
        got["y", j, 0].wait_recv()
        for d in range(1, H):
            got["xy", j, d].wait_recv()
            got["yx", j, d].wait_recv()
        got["c", j, 1] = same(rows_all.at[:, :, pl.ds(theirs, RB), :], to_c)

    def compute(j):
        zc = flip(z, j)
        start = block(zc, 0, 0)
        got["c", j, 0].wait_recv()
        got["c", j, 1].wait_recv()
        got["cw", j].wait_recv()
        if j == 0:
            fetches[0].wait()
            fetches[1].wait()
        gate = jnp.zeros((RC, w_gate.shape[1]), jnp.float32)
        up = gate
        for s in range(2 * H):
            a = rows_all[s // 2, s % 2, pl.ds(start, RC), :]
            gate = gate + jnp.dot(a, w_gate[s * WD:(s + 1) * WD, :], preferred_element_type=jnp.float32)
            up = up + jnp.dot(a, w_up[s * WD:(s + 1) * WD, :], preferred_element_type=jnp.float32)
        act[...] = (gate / (1.0 + jnp.exp(-gate)) * up).astype(jnp.bfloat16)
        if j == 0:
            for f in fetches[2:]:
                f.wait()
        lanes = lax.broadcasted_iota(jnp.int32, (RC, LANES), 1)
        scale = jnp.sum(jnp.where(lanes == me, table[pl.ds(start, RC), :], 0.0), axis=1, keepdims=True)
        for s in range(2 * H):
            o = jnp.dot(act[...], w_down[s // 2, s % 2], preferred_element_type=jnp.float32)
            part[j, s // 2, s % 2] = (o * scale).astype(jnp.bfloat16)
        away = pl.multiple_of(other * 2 * RB, 2 * RB)
        got["rc", j] = send(part.at[j, :, :, pl.ds(away, 2 * RB), :], d2d_in.at[j], to_c)

    home = pl.multiple_of(c * 2 * RB, 2 * RB)
    mine_at = pl.multiple_of((c * 2 + y) * RB, RB)
    theirs_at = pl.multiple_of((c * 2 + 1 - y) * RB, RB)

    def f32(v):
        return v.astype(jnp.float32)

    def r_first(j):
        got["rc", j].wait_recv()
        for s in range(2 * H):
            h, p = s // 2, s % 2
            v = f32(part[j, h, p, pl.ds(home, 2 * RB), :]) + f32(d2d_in[j, h, p])
            part[j, h, p, pl.ds(home, 2 * RB), :] = v.astype(jnp.bfloat16)
        got["ry", j] = send(part.at[j, :, 0, pl.ds(theirs_at, RB), :], y_in.at[j], to_y)
        for d in range(1, H):
            got["rx", j, d] = send(
                part.at[j, (x + d) % H, 1, pl.ds(home, 2 * RB), :], x_in.at[j, d - 1], to_x(d)
            )

    def r_second(j):
        got["ry", j].wait_recv()
        for h in range(H):
            v = f32(part[j, h, 0, pl.ds(mine_at, RB), :]) + f32(y_in[j, h])
            part[j, h, 0, pl.ds(mine_at, RB), :] = v.astype(jnp.bfloat16)
        for d in range(1, H):
            got["rx2", j, d] = send(
                part.at[j, (x + d) % H, 0, pl.ds(mine_at, RB), :], x_in2.at[j, d - 1], to_x(d)
            )
        v = f32(part[j, x, 1, pl.ds(home, 2 * RB), :])
        for d in range(1, H):
            got["rx", j, d].wait_recv()
            v = v + f32(x_in[j, d - 1])
        part[j, x, 1, pl.ds(home, 2 * RB), :] = v.astype(jnp.bfloat16)
        got["ry2", j] = send(part.at[j, x, 1, pl.ds(theirs_at, RB), :], y_in2.at[j], to_y)

    def r_third(j):
        v = f32(part[j, x, 0, pl.ds(mine_at, RB), :])
        for d in range(1, H):
            got["rx2", j, d].wait_recv()
            v = v + f32(x_in2[j, d - 1])
        z_out[j, 0] = v.astype(jnp.bfloat16)
        v = f32(part[j, x, 1, pl.ds(mine_at, RB), :])
        got["ry2", j].wait_recv()
        v = v + f32(y_in2[j])
        z_out[j, 1] = v.astype(jnp.bfloat16)
        if j == 3:
            got["rz", j] = send(z_out.at[j], z_in.at[j - 1], to_z(1))
        elif j and (j != 2 or Z <= 3):
            got["rz", j] = send(z_out.at[j], z_in.at[j - 1], to_z(j))

    def r_join(j):
        got["rz", 3].wait_recv()
        z_out[2] = (f32(z_out[2]) + f32(z_in[2])).astype(jnp.bfloat16)
        got["rz", 2] = send(z_out.at[2], z_in.at[1], to_z(2))

    steps = [(g_start, 0), (g_forward, 0), (g_start, 1)]
    for j in range(2, Z):
        steps += [(g_start, j), (g_forward, j - 1), (g_pair, j - 2)]
        steps += [(compute, j - 3), (r_first, j - 3), (r_second, j - 4), (r_third, j - 5)]
    n = Z - 1
    steps += [
        (g_forward, n), (compute, n - 2), (g_pair, n - 1), (r_first, n - 2), (r_second, n - 3),
        (compute, n - 1), (g_pair, n), (r_first, n - 1), (r_third, n - 4), (r_second, n - 2), (r_third, n - 3),
        (compute, n), (r_first, n), (r_third, n - 2), (r_second, n - 1),
    ]
    steps = [(f, j) for f, j in steps if j > 0 or (j == 0 and f not in (r_first, r_second, r_third))]
    steps += [
        (r_second, n), (r_first, 0), (r_third, n - 1), (r_third, n), (r_second, 0), (r_join, 0), (r_third, 0),
    ]
    for step, j in steps:
        step(j)

    direct = [j for j in range(1, Z) if j != 3]
    for j in direct:
        got["rz", j].wait_recv()
    for p in range(2):
        v = f32(z_out[0, p])
        for j in direct:
            v = v + f32(z_in[j - 1, p])
        out[:, p * WD:(p + 1) * WD] = v.astype(jnp.bfloat16)
    for copy in sent:
        copy.wait_send()


def body(hidden, ids, weights, w_gate, w_up, w_down):
    E = lax.axis_size("expert")
    H = lax.axis_size("head")
    Z = E // 2
    RB, DL = hidden.shape
    ids, weights = ids.T, weights.T
    WD = DL // 2
    D, F = w_gate.shape[1:]
    rows = E * 2 * RB
    copies = 8 * Z * (H + 2)
    vmem = pl.BlockSpec(memory_space=pltpu.VMEM)
    anyspace = pl.BlockSpec(memory_space=pl.ANY)
    bf16 = jnp.bfloat16
    X = max(H - 1, 1)
    return pl.pallas_call(
        functools.partial(kernel, (Z, H, RB)),
        out_shape=jax.ShapeDtypeStruct((RB, DL), bf16),
        in_specs=[vmem] * 3 + [anyspace] * 3,
        out_specs=vmem,
        scratch_shapes=[
            pltpu.VMEM((H, 2, rows, WD), bf16),
            pltpu.VMEM((rows, LANES), jnp.float32),
            pltpu.VMEM((LANES, LANES), jnp.float32),
            pltpu.VMEM((D, F), bf16),
            pltpu.VMEM((D, F), bf16),
            pltpu.VMEM((H, 2, F, WD), bf16),
            pltpu.VMEM((Z, H, 2, 4 * RB, WD), bf16),
            pltpu.VMEM((4 * RB, F), bf16),
            pltpu.VMEM((Z, H, 2, 2 * RB, WD), bf16),
            pltpu.VMEM((Z, H, RB, WD), bf16),
            pltpu.VMEM((Z, X, 2 * RB, WD), bf16),
            pltpu.VMEM((Z, X, RB, WD), bf16),
            pltpu.VMEM((Z, RB, WD), bf16),
            pltpu.VMEM((Z, 2, RB, WD), bf16),
            pltpu.VMEM((Z - 1, 2, RB, WD), bf16),
            pltpu.SemaphoreType.DMA((2 + 2 * H,)),
            pltpu.SemaphoreType.DMA((copies,)),
            pltpu.SemaphoreType.DMA((copies,)),
        ],
        compiler_params=pltpu.CompilerParams(
            collective_id=0, has_side_effects=True, vmem_limit_bytes=56 * 1024 * 1024
        ),
    )(hidden, ids, weights, w_gate, w_up, w_down)


def solution(mesh):
    return jax.shard_map(
        body,
        mesh=mesh,
        in_specs=(
            P(("groups", "expert", "pair"), "head"),
            P(("groups", "expert", "pair"), None),
            P(("groups", "expert", "pair"), None),
            P(("expert", "pair"), None, "head"),
            P(("expert", "pair"), None, "head"),
            P(("expert", "pair"), "head", None),
        ),
        out_specs=P(("groups", "expert", "pair"), "head"),
        check_vma=False,
    )
```
